512 devices in a mesh: af: 64 (over z, x, core), gx: 8 (over y).
Axes of the slice: x: 4, y: 8, z: 8, core: 2. Of those that a mesh axis runs over, the one named last changes fastest.
Arguments:
- volts: bfloat16 [1024, 128, 2, 1024], P('af', 'gx'), may hold values from -6 to 6
- history: bfloat16 [1024, 128, 2, 1408], P('af', 'gx'), may hold values from -6 to 6
- pfb_taps: float32 [12, 128], replicated, may hold values from -1.75 to 1.75
- zoom_bins: int32 [16384, 1], replicated, may hold values from 0 to 63, as said below
- counts: int32 [16384], replicated, may hold values from 1 to 8
- beam_stations: int32 [6, 256], replicated, may hold values from 0 to 511
- beam_weights: float32 [2, 6, 1024], replicated, may hold values from -0.125 to 0.125
Outputs:
- vis: bfloat16 [64, 8, 1024, 1024], P('af', 'gx')
- beam_power: float32 [6, 128, 128, 8], P(None, 'gx', 'af')
The draws below stay inside these ranges and needn't reach their ends.
Inputs may be any that keep to these rules, and one draw needn't show every extreme that they name: `zoom_bins`: within each aligned block of 2048 entries (one channel group) no bin is named by more than 64 channels; in every block one bin is named by exactly 64 channels and at least one bin by none. `beam_stations`: entries may repeat; a repeated station counts once for each entry.
All inputs are finite; a program needn't handle non-finite values.
Results may differ from the reference program's by a relative error of at most 0.0079.
Values may be sent and summed in bfloat16 or wider, within the bound.
A program may use at most 128 MiB of HBM per device.

```python
import jax
import jax.numpy as jnp
from jax import lax

STATIONS = 512
NIN = 1024
FINE = 128
TAPS = 12
NT = 8
NB = 6
SEL = 256
NCOARSE = 128
NCH = 16384
SUB = 16
CHG = 2048
BINS = 64
CAP = 64
N_GX = 8


def zoom_block(block_key):
    key_order, key_weight, key_break, key_shuffle = jax.random.split(block_key, 4)
    ranking = jax.random.permutation(key_order, jnp.arange(BINS, dtype=jnp.int32))
    full_bin = ranking[0]
    empty_bin = ranking[1]
    weights = jax.random.randint(key_weight, (BINS,), 1, 9, dtype=jnp.int32)
    tie_break = jax.random.permutation(key_break, jnp.arange(BINS * CAP, dtype=jnp.int32)).reshape(BINS, CAP)
    bin_ids = jnp.arange(BINS, dtype=jnp.int32)[:, None]
    slot_ids = jnp.arange(CAP, dtype=jnp.int32)[None, :]
    scores = weights[:, None] * (CAP - slot_ids) * (BINS * CAP) + tie_break
    scores = jnp.where(bin_ids == full_bin, jnp.int32(2 ** 30) - slot_ids, scores)
    scores = jnp.where(bin_ids == empty_bin, -1 - tie_break, scores)
    chosen = jnp.argsort(-scores.reshape(-1), stable=True)[:CHG].astype(jnp.int32)
    labels = (chosen // CAP).astype(jnp.int32)
    return jax.random.permutation(key_shuffle, labels).astype(jnp.int32)


def draw_zoom_bins(key, part):
    key = jax.random.fold_in(key, 11)
    block_keys = jax.random.split(key, NCH // CHG)
    labels = jax.vmap(zoom_block)(block_keys)
    return labels.reshape(NCH, 1).astype(jnp.int32)


def set_ends(entries, key, low, top_value):
    index_at = [jax.random.randint(jax.random.fold_in(key, axis), (), 0, length) for axis, length in enumerate(entries.shape)]
    widest = entries.shape.index(max(entries.shape))
    next_to = index_at[:widest] + [(index_at[widest] + 1) % entries.shape[widest]] + index_at[widest + 1:]
    return entries.at[tuple(index_at)].set(low).at[tuple(next_to)].set(top_value)


def level_of(rng, dims, shards, least, top_value):
    loudness, own = 1.0, jax.random.fold_in(rng, 6)
    for axis_at, shards_of in shards:
        draws = jnp.exp(jax.random.uniform(jax.random.fold_in(own, axis_at), (shards_of,), jnp.float32, least / len(shards), top_value / len(shards)))
        loudness = loudness * jnp.repeat(draws, dims[axis_at] // shards_of).reshape([-1 if axis == axis_at else 1 for axis in range(len(dims))])
    return loudness


def noise(own_key, dims, scale, bound, shards=(), kind=jnp.bfloat16):
    values = scale * jax.random.normal(own_key, dims, jnp.float32)
    if shards:
        values = values * level_of(own_key, dims, shards, -0.22, 0.18)
    return jnp.clip(values, -bound, bound).astype(kind)


def setup_inputs(seed: int = 0) -> dict:
    splits = jax.random.split(jax.random.key(seed), 8)
    return {
        "volts": noise(splits[0], (NIN, NCOARSE, 2, NT * FINE), 1.0, 6.0, ((0, 64), (1, 8))),
        "history": noise(splits[1], (NIN, NCOARSE, 2, (TAPS - 1) * FINE), 1.0, 6.0, ((0, 64), (1, 8))),
        "pfb_taps": noise(splits[2], (TAPS, FINE), TAPS ** -0.5, 1.75, (), jnp.float32),
        "zoom_bins": draw_zoom_bins(jax.random.fold_in(splits[7], 71), 0),
        "counts": set_ends(jax.random.randint(splits[4], (NCH,), 1, NT + 1), jax.random.fold_in(splits[4], 1), 1, NT).astype(jnp.int32),
        "beam_stations": set_ends(jax.random.randint(splits[5], (NB, SEL), 0, STATIONS), jax.random.fold_in(splits[5], 1), 0, STATIONS - 1).astype(jnp.int32),
        "beam_weights": noise(splits[6], (2, NB, NIN), (2 * NIN) ** -0.5, 0.125, (), jnp.float32),
    }


def dft_table(fine):
    index = jnp.arange(fine, dtype=jnp.int32)
    product = index[:, None] * index[None, :] % fine
    angle = product.astype(jnp.float32) * jnp.float32(2.0 * 3.141592653589793 / fine)
    cosine = jnp.cos(angle) / jnp.sqrt(jnp.float32(fine))
    sine = jnp.sin(angle) / jnp.sqrt(jnp.float32(fine))
    first_row = jnp.stack([cosine, -sine], 1)
    second_row = jnp.stack([sine, cosine], 1)
    return jnp.stack([first_row, second_row], 0).astype(jnp.bfloat16)

def channelize(extended, filter_taps, table):
    inputs_here, coarse, parts, length = extended.shape
    fine = filter_taps.shape[1]
    tap_count = filter_taps.shape[0]
    frames = extended.reshape(inputs_here, coarse, parts, length // fine, fine)
    steps = length // fine - tap_count + 1
    filtered = frames[:, :, :, 0:steps, :].astype(jnp.float32) * filter_taps[0]
    for offset in range(1, tap_count):
        filtered = filtered + frames[:, :, :, offset:offset + steps, :].astype(jnp.float32) * filter_taps[offset]
    filtered = filtered.astype(jnp.bfloat16)
    result = jnp.einsum('icrtn,rnsk->istck', filtered.astype(jnp.float32), table.astype(jnp.float32))
    return result.astype(jnp.bfloat16)

def beam_matrix(station_lists, weights, first_input, input_count):
    station_ids = (first_input + jnp.arange(input_count, dtype=jnp.int32)) // 2
    member = lax.optimization_barrier(jnp.sum((station_lists[:, :, None] == station_ids[None, None, :]).astype(jnp.float32), axis=1))
    chosen = lax.dynamic_slice_in_dim(weights, jnp.int32(first_input), input_count, 2)
    weight_re = (member * chosen[0]).T
    weight_im = (member * chosen[1]).T
    inner_first = jnp.stack([weight_re, weight_im], -1)
    inner_second = jnp.stack([-weight_im, weight_re], -1)
    return jnp.stack([inner_first, inner_second], 1).astype(jnp.bfloat16)

def slot_table(bins_group, bin_count, capacity):
    size = bins_group.shape[0]
    bin_ids = jnp.arange(bin_count, dtype=jnp.int32)
    hits = (bins_group[:, None] == bin_ids[None, :]).astype(jnp.int32)
    per_bin = lax.optimization_barrier(jnp.sum(hits, axis=0)).astype(jnp.int32)
    starts = (jnp.cumsum(per_bin) - per_bin).astype(jnp.int32)
    order = jnp.argsort(bins_group, stable=True).astype(jnp.int32)
    sorted_bins = jnp.take(bins_group, order).astype(jnp.int32)
    first = lax.optimization_barrier(jnp.sum(jnp.where(sorted_bins[:, None] == bin_ids[None, :], starts[None, :], 0), axis=1)).astype(jnp.int32)
    rank = jnp.arange(size, dtype=jnp.int32) - first
    target = (sorted_bins * capacity + rank).astype(jnp.int32)
    source = jnp.zeros((bin_count * capacity,), jnp.int32).at[target].set(order)
    filled = jnp.zeros((bin_count * capacity,), jnp.int32).at[target].set(jnp.ones((size,), jnp.int32))
    return (source.reshape(bin_count, capacity), filled.reshape(bin_count, capacity))

def reference(volts, history, pfb_taps, zoom_bins, counts, beam_stations, beam_weights):
    table = dft_table(FINE)
    extended = jnp.concatenate([history, volts], axis=3)
    blocks = extended.reshape((NIN // 64, 64) + extended.shape[1:])
    spectra = lax.map(lambda block: channelize(block, pfb_taps, table), blocks)
    spectra = spectra.reshape(NIN, 2, NT, NCOARSE, FINE)
    weights_eff = beam_matrix(beam_stations, beam_weights, 0, NIN).astype(jnp.float32)
    coarse_dev = NCOARSE // N_GX
    power_parts = []
    for block_index in range(N_GX):
        block_spectra = spectra[:, :, :, block_index * coarse_dev:(block_index + 1) * coarse_dev].astype(jnp.float32)
        beams = jnp.einsum('irtck,irbs->bsckt', block_spectra, weights_eff)
        power_parts.append(beams[:, 0] * beams[:, 0] + beams[:, 1] * beams[:, 1])
    beam_power = jnp.concatenate(power_parts, 1)
    row_ids = jnp.arange(NIN, dtype=jnp.int32)
    upper = row_ids[None, :] >= row_ids[:, None]
    time_ids = jnp.arange(NT, dtype=jnp.int32)
    vis_parts = []
    for group in range(N_GX):
        group_spectra = spectra[:, :, :, :, group * SUB:(group + 1) * SUB].reshape(NIN, 2, NT, CHG)
        bins_group = zoom_bins[group * CHG:(group + 1) * CHG, 0]
        counts_group = counts[group * CHG:(group + 1) * CHG]
        source, filled = slot_table(bins_group, BINS, CAP)

        def one_bin(bin_index):
            row_source = source[bin_index]
            row_filled = filled[bin_index]
            selected = jnp.take(group_spectra, row_source, axis=3).astype(jnp.float32)
            slot_counts = jnp.where(row_filled == 1, jnp.take(counts_group, row_source), 0)
            valid = time_ids[:, None] < slot_counts[None, :]
            masked = jnp.where(valid[None, None], selected, jnp.float32(0.0))
            flat = masked.reshape(NIN, 2 * NT * CAP)
            real_part = jnp.dot(flat, flat.T, precision=lax.Precision.HIGHEST)
            part_re = masked[:, 0].reshape(NIN, NT * CAP)
            part_im = masked[:, 1].reshape(NIN, NT * CAP)
            imag_part = jnp.dot(part_im, part_re.T, precision=lax.Precision.HIGHEST) - jnp.dot(part_re, part_im.T, precision=lax.Precision.HIGHEST)
            total = jnp.sum(jnp.where(bins_group == bin_index, counts_group, 0))
            scale = jnp.maximum(total, 1).astype(jnp.float32)
            return (jnp.where(upper, real_part, imag_part) / scale).astype(jnp.bfloat16)
        vis_parts.append(lax.map(one_bin, jnp.arange(BINS, dtype=jnp.int32)))
    vis = jnp.stack(vis_parts, 1)
    return (vis, beam_power)
```

```python
import jax
import jax.numpy as jnp
import numpy as np
from jax import lax
from jax.experimental import pallas as pl
from jax.experimental.pallas import tpu as pltpu
from jax.sharding import PartitionSpec as P

FINE = 128
TAPS = 12
NT = 8
NB = 6
BINS = 64
GROUPS = 8
LOCAL = 16
COARSE = 16
CHG = 2048
NIN = 1024
HALF = 4
LANES = 512
MESH = pl.DeviceIdType.MESH
CONTRACT_LANES = (((1,), (1,)), ((), ()))
CONTRACT_ROWS = (((0,), (0,)), ((), ()))


def dft_rows():
    index = np.arange(FINE)
    angle = (index[:, None] * index[None, :] % FINE) * (2.0 * np.pi / FINE)
    cosine = np.cos(angle) / np.sqrt(FINE)
    sine = np.sin(angle) / np.sqrt(FINE)
    return jnp.asarray(np.concatenate([cosine.T, sine.T], axis=1), jnp.bfloat16)


def to(device):
    return dict(device_id=device, device_id_type=MESH)


def kernel(
    volts, history, aux, table, taps, weights,
    vis, power,
    frames, filt, ysend, yrecv, pick, outgo, arrived, acc, visbuf,
    beams, bsend0, brecv0, bsend1, brecv1, bsend2, brecv2,
    frame_sem, ysend_sem, yrecv_sem, send_sem, recv_sem,
    bsend_sem, brecv_sem, vis_sem,
):
    me = lax.axis_index("af")
    gx = lax.axis_index("gx")
    my_z = me // 8
    my_x = (me // 2) % 4
    my_core = me % 2
    my_low = me % 8
    f32, bf16 = jnp.float32, jnp.bfloat16

    barrier = pltpu.get_barrier_semaphore()

    def greet(d, carry):
        pl.semaphore_signal(barrier, inc=1, **to({"af": (me + d) % BINS}))
        return carry

    lax.fori_loop(1, BINS, greet, 0)

    def greet_gx(d, carry):
        pl.semaphore_signal(barrier, inc=1, **to({"gx": (gx + d) % GROUPS}))
        return carry

    lax.fori_loop(1, GROUPS, greet_gx, 0)

    def fetch(i, carry):
        def old(f, c):
            cut = pl.ds(pl.multiple_of(f * FINE, FINE), FINE)
            pltpu.make_async_copy(history.at[i, :, :, cut], frames.at[:, f, i], frame_sem).start()
            return c

        lax.fori_loop(0, TAPS - 1, old, 0)

        def new(f, c):
            cut = pl.ds(pl.multiple_of(f * FINE, FINE), FINE)
            pltpu.make_async_copy(volts.at[i, :, :, cut], frames.at[:, TAPS - 1 + f, i], frame_sem).start()
            return c

        lax.fori_loop(0, NT, new, 0)
        return carry

    lax.fori_loop(0, LOCAL, fetch, 0)
    pltpu.make_async_copy(frames, frames, frame_sem).wait()

    frame_rows = frames.reshape(COARSE, NT + TAPS - 1, 2 * LOCAL, FINE)

    def channelize(half):
        def one(c, carry):
            for t in range(HALF):
                first = half * HALF + t
                total = frame_rows[c, first].astype(f32) * taps[0:1, :]
                for j in range(1, TAPS):
                    total = total + frame_rows[c, first + j].astype(f32) * taps[j : j + 1, :]
                filt[pl.ds(t * 2 * LOCAL, 2 * LOCAL), :] = total
            re = filt[pl.ds(0, HALF * LOCAL, stride=2), :].astype(bf16)
            im = filt[pl.ds(1, HALF * LOCAL, stride=2), :].astype(bf16)
            rows = jnp.concatenate(
                [jnp.concatenate([re, im], axis=1), jnp.concatenate([im, -re], axis=1)], axis=0
            )
            spectra = lax.dot_general(
                table[...], rows, CONTRACT_LANES, preferred_element_type=f32
            ).astype(bf16)
            ysend[half, :, c] = spectra.reshape(GROUPS, 16, FINE)
            part = jnp.dot(spectra, weights[half], preferred_element_type=f32)
            spot = pl.ds(c, FINE, stride=COARSE)
            if half == 0:
                beams[spot, :] = part
            else:
                beams[spot, :] = beams[spot, :] + part
            return carry

        lax.fori_loop(0, COARSE, one, 0)

    def send_spectra(half):
        def one(d, carry):
            dest = (gx + d) % GROUPS
            pltpu.make_async_remote_copy(
                src_ref=ysend.at[half, dest],
                dst_ref=yrecv.at[half, gx],
                send_sem=ysend_sem.at[half],
                recv_sem=yrecv_sem.at[half],
                **to({"gx": dest}),
            ).start()
            return carry

        lax.fori_loop(1, GROUPS, one, 0)
        yrecv[half, gx] = ysend[half, gx]

    channelize(0)
    pl.semaphore_wait(barrier, BINS - 1 + GROUPS - 1)
    send_spectra(0)
    channelize(1)
    send_spectra(1)

    def pack0(s, carry):
        row = pl.multiple_of((s * 2 + 1 - my_core) * 32, 32)
        bsend0[s] = beams[pl.ds(row, 32), :].astype(bf16)
        return carry

    lax.fori_loop(0, 32, pack0, 0)
    sibling = my_z * 8 + my_x * 2 + 1 - my_core
    core_copy = pltpu.make_async_remote_copy(
        src_ref=bsend0, dst_ref=brecv0, send_sem=bsend_sem.at[0], recv_sem=brecv_sem.at[0],
        **to({"af": sibling}),
    )
    core_copy.start()

    lane = lax.broadcasted_iota(jnp.int32, (256, FINE), 1)
    lower = (
        lax.broadcasted_iota(jnp.int32, (256, 256), 1) < lax.broadcasted_iota(jnp.int32, (256, 256), 0)
    ).astype(f32).astype(bf16)

    def place(block, seen):
        rows = pl.ds(pl.multiple_of(block * 256, 256), 256)
        hits = jnp.where(lane < BINS, aux[rows, :].astype(f32), 0.0)
        before = jnp.dot(lower, hits.astype(bf16), preferred_element_type=f32) + seen
        target = jnp.sum(hits * (before + (lane * 64).astype(f32)), axis=1, keepdims=True)
        target = jnp.broadcast_to(target, (256, FINE)).astype(jnp.int32)

        def column(z, carry):
            for p in range(4):
                here = lane + (z * 512 + p * FINE)
                pick[z, rows, p * FINE : (p + 1) * FINE] = (target == here).astype(f32).astype(bf16)
            return carry

        lax.fori_loop(0, 8, column, 0)
        return seen + jnp.sum(hits, axis=0, keepdims=True)

    lax.fori_loop(0, CHG // 256, place, jnp.zeros((1, FINE), f32))

    tally = lax.dot_general(aux[...], aux[...], CONTRACT_ROWS, preferred_element_type=f32)
    row_id = lax.broadcasted_iota(jnp.int32, (FINE, FINE), 0)
    col_id = lax.broadcasted_iota(jnp.int32, (FINE, FINE), 1)
    mine = jnp.logical_and(row_id == me, jnp.logical_and(col_id >= 64, col_id < 64 + NT))
    count = jnp.sum(jnp.where(mine, tally, 0.0), axis=1, keepdims=True)
    count = jnp.sum(count, axis=0, keepdims=True)
    scale = 1.0 / jnp.maximum(count, 1.0)

    def distribute(half):
        pltpu.make_async_copy(
            yrecv.at[half, pl.ds(0, GROUPS - 1)], yrecv.at[half, pl.ds(0, GROUPS - 1)], yrecv_sem.at[half]
        ).wait()
        spread = (row_id == 64 + half * HALF + (col_id // LOCAL) % HALF).astype(f32).astype(bf16)
        valid = jnp.dot(aux[...], spread, preferred_element_type=f32)
        samples = yrecv[half].reshape(CHG, FINE).astype(f32)
        flipped = jnp.where(valid > 0.5, samples, 0.0).T.astype(bf16)
        low = lax.broadcasted_iota(jnp.int32, (LOCAL, FINE), 1) < 64

        def one(step, carry):
            turn = 7 - step
            hop = ((turn + 1) // 2) * (2 * (turn % 2) - 1)
            z = (my_z + hop + 8) % 8
            picked = jnp.dot(flipped, pick[z], preferred_element_type=f32)
            for pair in range(4):
                for s in range(2):
                    for tp in range(2):
                        row = s * 64 + tp * 32
                        first = picked[row : row + 16, pair * FINE : (pair + 1) * FINE]
                        second = picked[row + 16 : row + 32, pair * FINE : (pair + 1) * FINE]
                        second = pltpu.roll(second, 64, 1)
                        cols = slice((s * 2 + tp) * FINE, (s * 2 + tp + 1) * FINE)
                        outgo[half, z * 8 + 2 * pair, :, cols] = jnp.where(low, first, second).astype(bf16)
                        outgo[half, z * 8 + 2 * pair + 1, :, cols] = jnp.where(low, second, first).astype(bf16)

            def send(k, c):
                dest = z * 8 + (my_low + k) % 8

                @pl.when(dest != me)
                def _():
                    pltpu.make_async_remote_copy(
                        src_ref=outgo.at[half, dest],
                        dst_ref=arrived.at[half, pl.ds(pl.multiple_of(me * LOCAL, LOCAL), LOCAL)],
                        send_sem=send_sem.at[half],
                        recv_sem=recv_sem.at[half],
                        **to({"af": dest}),
                    ).start()

                return c

            lax.fori_loop(0, 8, send, 0)
            return carry

        lax.fori_loop(0, 8, one, 0)
        arrived[half, pl.ds(pl.multiple_of(me * LOCAL, LOCAL), LOCAL)] = outgo[half, me]

    def correlate(half):
        others = pl.ds(0, (BINS - 1) * LOCAL)
        pltpu.make_async_copy(arrived.at[half, others], arrived.at[half, others], recv_sem.at[half]).wait()

        def stripe(bi, carry):
            rows = pl.ds(pl.multiple_of(bi * 256, 256), 256)
            left = arrived[half, rows, :]
            turned = jnp.concatenate([left[:, 256:], -left[:, :256]], axis=1)

            def block(bj, c):
                cols = pl.ds(pl.multiple_of(bj * 256, 256), 256)
                right = arrived[half, cols, :]

                def finish(value):
                    if half == 0:
                        acc[bi, bj] = value
                    else:
                        visbuf[rows, cols] = ((acc[bi, bj] + value) * scale).astype(bf16)

                @pl.when(bj > bi)
                def _():
                    finish(lax.dot_general(left, right, CONTRACT_LANES, preferred_element_type=f32))

                @pl.when(bj < bi)
                def _():
                    finish(lax.dot_general(turned, right, CONTRACT_LANES, preferred_element_type=f32))

                @pl.when(bj == bi)
                def _():
                    real = lax.dot_general(left, right, CONTRACT_LANES, preferred_element_type=f32)
                    imag = lax.dot_general(turned, right, CONTRACT_LANES, preferred_element_type=f32)
                    upper = lax.broadcasted_iota(jnp.int32, (256, 256), 1) >= lax.broadcasted_iota(
                        jnp.int32, (256, 256), 0
                    )
                    finish(jnp.where(upper, real, imag))

                return c

            lax.fori_loop(0, 4, block, 0)
            if half == 1:
                pltpu.make_async_copy(visbuf.at[rows], vis.at[rows], vis_sem).start()
            return carry

        lax.fori_loop(0, 4, stripe, 0)

    distribute(0)

    core_copy.wait()

    def pack1(s, carry):
        row = pl.multiple_of((s * 2 + my_core) * 32, 32)
        total = beams[pl.ds(row, 32), :] + brecv0[s].astype(f32)
        beams[pl.ds(row, 32), :] = total
        bsend1[s % 4, s // 4] = total.astype(bf16)
        return carry

    lax.fori_loop(0, 32, pack1, 0)
    x_copies = []
    for d in range(1, 4):
        x = (my_x + d) % 4
        x_copies.append(
            pltpu.make_async_remote_copy(
                src_ref=bsend1.at[x], dst_ref=brecv1.at[d - 1],
                send_sem=bsend_sem.at[d], recv_sem=brecv_sem.at[d],
                **to({"af": my_z * 8 + x * 2 + my_core}),
            )
        )
        x_copies[-1].start()

    distribute(1)

    for copy in x_copies:
        copy.wait()

    def pack2(zz, carry):
        row = pl.multiple_of(((zz * 4 + my_x) * 2 + my_core) * 32, 32)
        total = beams[pl.ds(row, 32), :]
        for d in range(3):
            total = total + brecv1[d, zz].astype(f32)
        beams[pl.ds(row, 32), :] = total
        bsend2[zz] = total.astype(bf16)
        return carry

    lax.fori_loop(0, 8, pack2, 0)
    z_copies = []
    for d in range(1, 8):
        zz = (my_z + d) % 8
        z_copies.append(
            pltpu.make_async_remote_copy(
                src_ref=bsend2.at[zz], dst_ref=brecv2.at[d - 1],
                send_sem=bsend_sem.at[3 + d], recv_sem=brecv_sem.at[3 + d],
                **to({"af": zz * 8 + my_low}),
            )
        )
        z_copies[-1].start()

    correlate(0)

    for copy in z_copies:
        copy.wait()
    total = beams[pl.ds(pl.multiple_of(me * 32, 32), 32), :]
    for d in range(7):
        total = total + brecv2[d].astype(f32)
    square = total * total
    power[...] = square + pltpu.roll(square, 64, 1)

    correlate(1)
    for half in range(2):
        pltpu.make_async_copy(
            ysend.at[half, pl.ds(0, GROUPS - 1)], ysend.at[half, pl.ds(0, GROUPS - 1)], ysend_sem.at[half]
        ).wait()
        others = pl.ds(0, BINS - 1)
        pltpu.make_async_copy(outgo.at[half, others], outgo.at[half, others], send_sem.at[half]).wait()
    pltpu.make_async_copy(visbuf, vis, vis_sem).wait()


def beam_matrix(stations, weights, first_input):
    ids = (first_input + jnp.arange(LOCAL, dtype=jnp.int32)) // 2
    member = jnp.sum((stations[:, :, None] == ids[None, None, :]).astype(jnp.float32), axis=1)
    chosen = lax.dynamic_slice_in_dim(weights, first_input, LOCAL, 2)
    w = (member[None] * chosen).astype(jnp.bfloat16)
    w = jnp.pad(w, ((0, 0), (0, 8 - NB), (0, 0)))
    table = jnp.stack([jnp.stack([w[0], w[1]], 0), jnp.stack([-w[1], w[0]], 0)], 0)
    same = (jnp.arange(2 * HALF)[:, None] == jnp.arange(NT)[None, :]).reshape(2, 1, HALF, 1, 1, NT, 1)
    body = table.transpose(0, 3, 1, 2)[None, :, None, :, :, None, :]
    full = jnp.where(same, body, jnp.zeros((), jnp.bfloat16))
    return full.reshape(2, FINE, FINE)


def per_device(volts, history, pfb_taps, zoom_bins, counts, beam_stations, beam_weights):
    me = lax.axis_index("af")
    group = lax.axis_index("gx")
    bins_here = lax.dynamic_slice_in_dim(zoom_bins[:, 0], group * CHG, CHG)
    counts_here = lax.dynamic_slice_in_dim(counts, group * CHG, CHG)
    lane = jnp.arange(FINE, dtype=jnp.int32)[None, :]
    aux = jnp.where(
        lane < BINS,
        bins_here[:, None] == lane,
        jnp.logical_and(lane < 64 + NT, lane - 64 < counts_here[:, None]),
    ).astype(jnp.bfloat16)
    weights = beam_matrix(beam_stations, beam_weights, me * LOCAL)
    vmem = pl.BlockSpec(memory_space=pltpu.VMEM)
    hbm = pl.BlockSpec(memory_space=pl.ANY)
    bf16, f32 = jnp.bfloat16, jnp.float32
    dma = pltpu.SemaphoreType.DMA
    vis, power = pl.pallas_call(
        kernel,
        out_shape=[
            jax.ShapeDtypeStruct((NIN, NIN), bf16),
            jax.ShapeDtypeStruct((32, FINE), f32),
        ],
        in_specs=[hbm, hbm, vmem, vmem, vmem, vmem],
        out_specs=[hbm, vmem],
        scratch_shapes=[
            pltpu.VMEM((COARSE, NT + TAPS - 1, LOCAL, 2, FINE), bf16),
            pltpu.VMEM((HALF * 2 * LOCAL, FINE), f32),
            pltpu.VMEM((2, GROUPS, COARSE, 16, FINE), bf16),
            pltpu.VMEM((2, GROUPS, COARSE, 16, FINE), bf16),
            pltpu.VMEM((8, CHG, 512), bf16),
            pltpu.VMEM((2, BINS, LOCAL, LANES), bf16),
            pltpu.VMEM((2, NIN, LANES), bf16),
            pltpu.VMEM((4, 4, 256, 256), f32),
            pltpu.VMEM((NIN, NIN), bf16),
            pltpu.VMEM((CHG, FINE), f32),
            pltpu.VMEM((32, 32, FINE), bf16),
            pltpu.VMEM((32, 32, FINE), bf16),
            pltpu.VMEM((4, 8, 32, FINE), bf16),
            pltpu.VMEM((3, 8, 32, FINE), bf16),
            pltpu.VMEM((8, 32, FINE), bf16),
            pltpu.VMEM((7, 32, FINE), bf16),
            dma,
            dma((2,)),
            dma((2,)),
            dma((2,)),
            dma((2,)),
            dma((11,)),
            dma((11,)),
            dma,
        ],
        compiler_params=pltpu.CompilerParams(
            collective_id=0, has_side_effects=True, vmem_limit_bytes=56 * 1024 * 1024
        ),
    )(volts, history, aux, dft_rows(), pfb_taps, weights)
    beam_power = power[:, :64].reshape(2, COARSE, NT, 8)[..., :NB].transpose(3, 1, 0, 2)
    return vis[None, None], beam_power


def solution(mesh):
    in_specs = (P("af", "gx", None, None), P("af", "gx", None, None), P(), P(), P(), P(), P())
    out_specs = (P("af", "gx", None, None), P(None, "gx", "af", None))
    return jax.shard_map(
        per_device, mesh=mesh, in_specs=in_specs, out_specs=out_specs, check_vma=False
    )
```

```python
import jax
import jax.numpy as jnp
import numpy as np
from jax import lax
from jax.experimental import pallas as pl
from jax.experimental.pallas import tpu as pltpu
from jax.sharding import PartitionSpec as P

FINE = 128
TAPS = 12
NT = 8
NB = 6
BINS = 64
GROUPS = 8
LOCAL = 16
COARSE = 16
CHG = 2048
NIN = 1024
STEPS = 4
LANES = 256
MESH = pl.DeviceIdType.MESH
CONTRACT_LANES = (((1,), (1,)), ((), ()))


def dft_rows():
    index = np.arange(FINE)
    angle = (index[:, None] * index[None, :] % FINE) * (2.0 * np.pi / FINE)
    cosine = np.cos(angle) / np.sqrt(FINE)
    sine = np.sin(angle) / np.sqrt(FINE)
    return jnp.asarray(np.concatenate([cosine.T, sine.T], axis=1), jnp.bfloat16)


def to(device):
    return dict(device_id=device, device_id_type=MESH)


def iota(shape, dim):
    return lax.broadcasted_iota(jnp.int32, shape, dim)


def kernel(
    volts, history, zoom_bins, counts, table, taps, stations, beam_weights,
    vis, power,
    frames, filt, ysend, yrecv, place, pick, limit, outgo, arrived, turned, acc, visbuf,
    wpad, beams, beams2, bsend0, brecv0, bsend1, brecv1, bsend2, brecv2,
    frame_sem, ysend_sem, yrecv_sem, send_sem, recv_sem,
    bsend_sem, brecv_sem, vis_sem,
):
    me = lax.axis_index("af")
    gx = lax.axis_index("gx")
    my_z = me // 8
    my_x = (me // 2) % 4
    my_core = me % 2
    my_low = me % 8
    f32, bf16 = jnp.float32, jnp.bfloat16

    barrier = pltpu.get_barrier_semaphore()

    def first_frame(step):
        return 0 if step == 0 else 11 + 2 * step

    def fetch_step(step):
        def one(i, carry):
            for f in range(first_frame(step), 13 + 2 * step):
                cut_fetch(f, i, step)
            return carry

        lax.fori_loop(0, LOCAL, one, 0)

    def cut_fetch(f, i, step):
        if f < TAPS - 1:
            source = history.at[i, :, :, f * FINE : (f + 1) * FINE]
        else:
            source = volts.at[i, :, :, (f - TAPS + 1) * FINE : (f - TAPS + 2) * FINE]
        pltpu.make_async_copy(source, frames.at[f, :, pl.ds(2 * i, 2)], frame_sem.at[step]).start()

    fetch_step(0)

    def greet(d, carry):
        pl.semaphore_signal(barrier, inc=1, **to({"af": (me + d) % BINS}))
        return carry

    lax.fori_loop(1, BINS, greet, 0)

    def greet_gx(d, carry):
        pl.semaphore_signal(barrier, inc=1, **to({"gx": (gx + d) % GROUPS}))
        return carry

    lax.fori_loop(1, GROUPS, greet_gx, 0)
    for step in range(1, STEPS):
        fetch_step(step)

    def channelize(step):
        cut = frames.at[first_frame(step) : 13 + 2 * step]
        pltpu.make_async_copy(cut, cut, frame_sem.at[step]).wait()

        def bank(c, carry):
            for part in range(2):
                rows = slice(part * LOCAL, (part + 1) * LOCAL)
                x = [frames[2 * step + j, c, rows, :].astype(f32) for j in range(TAPS + 1)]
                for t in range(2):
                    total = x[t] * taps[0:1, :]
                    for j in range(1, TAPS):
                        total = total + x[t + j] * taps[j : j + 1, :]
                    filt[c, t * 32 + part * LOCAL : t * 32 + (part + 1) * LOCAL, :] = total
            return carry

        lax.fori_loop(0, COARSE, bank, 0, unroll=2)

        def transform(u, carry):
            blocks = []
            for cp in range(2):
                for upper in range(2):
                    c = 2 * u + cp + 8 * upper
                    re = filt[c, pl.ds(0, 32, stride=2), :].astype(bf16)
                    im = filt[c, pl.ds(1, 32, stride=2), :].astype(bf16)
                    blocks.append(jnp.concatenate([re, im], axis=1))
                    blocks.append(jnp.concatenate([im, -re], axis=1))
            rows = jnp.concatenate(blocks, axis=0)
            spectra = lax.dot_general(table[...], rows, CONTRACT_LANES, preferred_element_type=f32).astype(bf16)
            for cp in range(2):
                ysend[step, :, 2 * u + cp] = spectra[:, cp * FINE : (cp + 1) * FINE].reshape(GROUPS, 16, FINE)
            return carry

        lax.fori_loop(0, 4, transform, 0, unroll=2)

    def send_spectra(step):
        def one(d, carry):
            dest = (gx + d) % GROUPS
            pltpu.make_async_remote_copy(
                src_ref=ysend.at[step, dest],
                dst_ref=yrecv.at[step, gx],
                send_sem=ysend_sem.at[step],
                recv_sem=yrecv_sem.at[step],
                **to({"gx": dest}),
            ).start()
            return carry

        lax.fori_loop(1, GROUPS, one, 0)
        yrecv[step, gx] = ysend[step, gx]

    channelize(0)
    pl.semaphore_wait(barrier, BINS - 1 + GROUPS - 1)
    send_spectra(0)
    channelize(1)
    send_spectra(1)

    my_rows = pl.ds(pl.multiple_of(gx * 16, 16), 16)
    bins_here = zoom_bins[my_rows, :]
    counts_here = counts[my_rows, :]
    in_bin = jnp.where(bins_here == me, counts_here.astype(f32), 0.0)
    in_bin = jnp.sum(jnp.sum(in_bin, axis=1, keepdims=True), axis=0, keepdims=True)
    scale = 1.0 / jnp.maximum(in_bin, 1.0)
    bins_down = bins_here.astype(f32).T
    counts_down = counts_here.astype(f32).T
    lane = iota((FINE, FINE), 1)
    lane_f = lane.astype(f32)
    lower = (lane < iota((FINE, FINE), 0)).astype(f32).astype(bf16)
    ones = jnp.ones((FINE, FINE), bf16)
    seen = jnp.zeros((1, FINE), f32)
    for block in range(16):
        upper, y = block // 8, block % 8
        row = 2 * y + upper
        column = jnp.broadcast_to(bins_down[:, row : row + 1], (FINE, FINE))
        hits = (column == lane_f).astype(f32)
        before = jnp.dot(lower, hits.astype(bf16), preferred_element_type=f32) + seen
        seen = seen + jnp.sum(hits, axis=0, keepdims=True)
        rank = jnp.dot((hits * before).astype(bf16), ones, preferred_element_type=f32)
        pair = jnp.floor(column * 0.5)
        slot = (column - 2.0 * pair) * 64.0 + rank
        place[block * FINE : (block + 1) * FINE, :] = jnp.where(slot == lane_f, pair, -1.0).astype(bf16)

    def spread(z, carry):
        for p in range(4):
            here = (z * 4 + p).astype(f32).astype(bf16)
            pick[z, :, p * FINE : (p + 1) * FINE] = jnp.where(
                place[...] == here, jnp.ones((), bf16), jnp.zeros((), bf16)
            )
        return carry

    lax.fori_loop(0, 8, spread, 0)
    for y in range(8):
        first = jnp.broadcast_to(counts_down[:, 2 * y : 2 * y + 1], (FINE, FINE))
        second = jnp.broadcast_to(counts_down[:, 2 * y + 1 : 2 * y + 2], (FINE, FINE))
        limit[y * FINE : (y + 1) * FINE, :] = jnp.where(lane < 64, first, second)

    own_rows = pl.ds(pl.multiple_of(me * LOCAL, LOCAL), LOCAL)

    def distribute(step):
        others = pl.ds(0, GROUPS - 1)
        pltpu.make_async_copy(yrecv.at[step, others], yrecv.at[step, others], yrecv_sem.at[step]).wait()
        spectrum = 2 * step + (iota((FINE, FINE), 1) // LOCAL) % 2
        pieces = []
        for y in range(GROUPS):
            samples = yrecv[step, y].reshape(FINE, FINE).astype(f32)
            keep = spectrum.astype(f32) < limit[y * FINE : (y + 1) * FINE, :]
            pieces.append(jnp.where(keep, samples, 0.0).T.astype(bf16))
        flipped = jnp.concatenate([p[:64] for p in pieces] + [p[64:] for p in pieces], axis=1)
        low = iota((LOCAL, FINE), 1) < 64

        def one(turn, carry):
            turn = 7 - turn
            hop = ((turn + 1) // 2) * (2 * (turn % 2) - 1)
            z = (my_z + hop + 8) % 8
            picked = jnp.dot(flipped, pick[z], preferred_element_type=f32)
            for pair in range(4):
                for s in range(2):
                    first = picked[s * 32 : s * 32 + 16, pair * FINE : (pair + 1) * FINE]
                    second = picked[s * 32 + 16 : s * 32 + 32, pair * FINE : (pair + 1) * FINE]
                    second = pltpu.roll(second, 64, 1)
                    cols = slice(s * FINE, (s + 1) * FINE)
                    outgo[step, z * 8 + 2 * pair, :, cols] = jnp.where(low, first, second).astype(bf16)
                    outgo[step, z * 8 + 2 * pair + 1, :, cols] = jnp.where(low, second, first).astype(bf16)

            def send(k, c):
                dest = z * 8 + (my_low + k) % 8

                @pl.when(dest != me)
                def _():
                    pltpu.make_async_remote_copy(
                        src_ref=outgo.at[step, dest],
                        dst_ref=arrived.at[step, own_rows],
                        send_sem=send_sem.at[step],
                        recv_sem=recv_sem.at[step],
                        **to({"af": dest}),
                    ).start()

                return c

            lax.fori_loop(0, 8, send, 0)
            return carry

        lax.fori_loop(0, 8, one, 0, unroll=8)
        arrived[step, own_rows] = outgo[step, me]

    distribute(0)
    channelize(2)
    send_spectra(2)
    channelize(3)
    send_spectra(3)
    distribute(1)

    lanes6 = iota((NB, FINE), 1)
    member = jnp.zeros((NB, FINE), f32)
    for st in range(LOCAL // 2):
        found = jnp.sum((stations[...] == me * (LOCAL // 2) + st).astype(f32), axis=1, keepdims=True)
        member = jnp.where(lanes6 // 2 == st, found, member)
    wpad[...] = jnp.zeros_like(wpad)
    for p in range(2):
        piece = beam_weights[p, :, pl.ds(pl.multiple_of((me // 8) * FINE, FINE), FINE)]
        piece = pltpu.roll(piece, (FINE - my_low * LOCAL) % FINE, 1)
        wpad[p * 8 : p * 8 + NB, :] = member * piece
    by_input = (iota((512, FINE), 1) == iota((512, FINE), 0) % LOCAL).astype(f32).astype(bf16)
    chosen = lax.dot_general(by_input, wpad[...].astype(bf16), CONTRACT_LANES, preferred_element_type=f32)
    chosen = chosen.astype(bf16)
    wide_row, wide_lane = iota((16, 256), 0), iota((16, 256), 1)
    wre = jnp.dot(chosen, (wide_row == wide_lane % 8).astype(f32).astype(bf16), preferred_element_type=f32)
    wim = jnp.dot(chosen, (wide_row == 8 + wide_lane % 8).astype(f32).astype(bf16), preferred_element_type=f32)
    row, col = iota((512, 256), 0), iota((512, 256), 1)
    s_of, part_of = (row // 32) % 2, (col // 64) % 2
    same = jnp.logical_and(
        (row // 64) % 2 == col // 128, 2 * (row // 128) + (row // LOCAL) % 2 == (col // 8) % 8
    )
    mixed = jnp.where(s_of == part_of, wre, jnp.where(s_of == 0, wim, -wim))
    weights = jnp.where(same, mixed, 0.0).astype(bf16)
    for z in range(8):
        spectra = jnp.concatenate([ysend[step, z].reshape(FINE, FINE) for step in range(STEPS)], axis=1)
        whole = jnp.dot(spectra, weights, preferred_element_type=f32)
        beams[0] = whole[:, :FINE]
        beams[1] = whole[:, FINE:]
        for x in range(4):
            for core in range(2):
                for e in range(2):
                    for h in range(2):
                        beams2[z, x, core, e * 8 : e * 8 + 8, h * FINE : (h + 1) * FINE] = beams[
                            h, pl.ds(x * 4 + core * 2 + e, 8, stride=16), :
                        ]

    def pack0(s, carry):
        bsend0[s] = beams2[s // 4, s % 4, 1 - my_core].astype(bf16)
        return carry

    lax.fori_loop(0, 32, pack0, 0)
    sibling = my_z * 8 + my_x * 2 + 1 - my_core
    core_copy = pltpu.make_async_remote_copy(
        src_ref=bsend0, dst_ref=brecv0, send_sem=bsend_sem.at[0], recv_sem=brecv_sem.at[0],
        **to({"af": sibling}),
    )
    core_copy.start()

    distribute(2)

    core_copy.wait()

    def pack1(s, carry):
        total = beams2[s // 4, s % 4, my_core] + brecv0[s].astype(f32)
        beams2[s // 4, s % 4, my_core] = total
        bsend1[s % 4, s // 4] = total.astype(bf16)
        return carry

    lax.fori_loop(0, 32, pack1, 0)
    x_copies = []
    for d in range(1, 4):
        x = (my_x + d) % 4
        x_copies.append(
            pltpu.make_async_remote_copy(
                src_ref=bsend1.at[x], dst_ref=brecv1.at[d - 1],
                send_sem=bsend_sem.at[d], recv_sem=brecv_sem.at[d],
                **to({"af": my_z * 8 + x * 2 + my_core}),
            )
        )
        x_copies[-1].start()

    distribute(3)

    for copy in x_copies:
        copy.wait()

    def pack2(zz, carry):
        total = beams2[zz, my_x, my_core]
        for d in range(3):
            total = total + brecv1[d, zz].astype(f32)
        beams2[zz, my_x, my_core] = total
        bsend2[zz] = total.astype(bf16)
        return carry

    lax.fori_loop(0, 8, pack2, 0)
    z_copies = []
    for d in range(1, 8):
        zz = (my_z + d) % 8
        z_copies.append(
            pltpu.make_async_remote_copy(
                src_ref=bsend2.at[zz], dst_ref=brecv2.at[d - 1],
                send_sem=bsend_sem.at[3 + d], recv_sem=brecv_sem.at[3 + d],
                **to({"af": zz * 8 + my_low}),
            )
        )
        z_copies[-1].start()

    diagonal = iota((256, 256), 1) >= iota((256, 256), 0)

    def correlate(step, last):
        others = pl.ds(0, (BINS - 1) * LOCAL)
        pltpu.make_async_copy(arrived.at[step, others], arrived.at[step, others], recv_sem.at[step]).wait()
        turned[:, :FINE] = arrived[step, :, FINE:]
        turned[:, FINE:] = -arrived[step, :, :FINE]
        for bi in range(4):
            rows = slice(bi * 256, (bi + 1) * 256)
            for bj in range(4):
                cols = slice(bj * 256, (bj + 1) * 256)
                right = arrived[step, cols, :]
                if bj >= bi:
                    real = lax.dot_general(
                        arrived[step, rows, :], right, CONTRACT_LANES, preferred_element_type=f32
                    )
                if bj <= bi:
                    imag = lax.dot_general(turned[rows, :], right, CONTRACT_LANES, preferred_element_type=f32)
                if bj > bi:
                    value = real
                elif bj < bi:
                    value = imag
                else:
                    value = jnp.where(diagonal, real, imag)
                if last:
                    visbuf[rows, cols] = ((acc[bi, bj] + value) * scale).astype(bf16)
                else:
                    acc[bi, bj] = acc[bi, bj] + value
            if last:
                pltpu.make_async_copy(visbuf.at[rows], vis.at[rows], vis_sem).start()

    def clear(k, carry):
        acc[k // 4, k % 4] = jnp.zeros((256, 256), f32)
        return carry

    lax.fori_loop(0, 16, clear, 0)

    def early(step, carry):
        correlate(step, False)
        return carry

    lax.fori_loop(0, STEPS - 1, early, 0)

    for copy in z_copies:
        copy.wait()
    total = beams2[my_z, my_x, my_core]
    for d in range(7):
        total = total + brecv2[d].astype(f32)
    square = total * total
    for h in range(2):
        half = square[:, h * FINE : (h + 1) * FINE]
        power[:, h * FINE : (h + 1) * FINE] = half + pltpu.roll(half, 64, 1)

    correlate(STEPS - 1, True)
    for step in range(STEPS):
        others = pl.ds(0, GROUPS - 1)
        pltpu.make_async_copy(ysend.at[step, others], ysend.at[step, others], ysend_sem.at[step]).wait()
        others = pl.ds(0, BINS - 1)
        pltpu.make_async_copy(outgo.at[step, others], outgo.at[step, others], send_sem.at[step]).wait()
    pltpu.make_async_copy(visbuf, vis, vis_sem).wait()


def per_device(volts, history, pfb_taps, zoom_bins, counts, beam_stations, beam_weights):
    vmem = pl.BlockSpec(memory_space=pltpu.VMEM)
    hbm = pl.BlockSpec(memory_space=pl.ANY)
    bf16, f32 = jnp.bfloat16, jnp.float32
    dma = pltpu.SemaphoreType.DMA
    vis, power = pl.pallas_call(
        kernel,
        out_shape=[
            jax.ShapeDtypeStruct((NIN, NIN), bf16),
            jax.ShapeDtypeStruct((16, 2 * FINE), f32),
        ],
        in_specs=[hbm, hbm, vmem, vmem, vmem, vmem, vmem, vmem],
        out_specs=[hbm, vmem],
        scratch_shapes=[
            pltpu.VMEM((NT + TAPS - 1, COARSE, 2 * LOCAL, FINE), bf16),
            pltpu.VMEM((COARSE, 64, FINE), f32),
            pltpu.VMEM((STEPS, GROUPS, 8, 16, FINE), bf16),
            pltpu.VMEM((STEPS, GROUPS, 8, 16, FINE), bf16),
            pltpu.VMEM((CHG, FINE), bf16),
            pltpu.VMEM((8, CHG, 512), bf16),
            pltpu.VMEM((CHG // 2, FINE), f32),
            pltpu.VMEM((STEPS, BINS, LOCAL, LANES), bf16),
            pltpu.VMEM((STEPS, NIN, LANES), bf16),
            pltpu.VMEM((NIN, LANES), bf16),
            pltpu.VMEM((4, 4, 256, 256), f32),
            pltpu.VMEM((NIN, NIN), bf16),
            pltpu.VMEM((16, FINE), f32),
            pltpu.VMEM((2, FINE, FINE), f32),
            pltpu.VMEM((8, 4, 2, 16, 256), f32),
            pltpu.VMEM((32, 16, 256), bf16),
            pltpu.VMEM((32, 16, 256), bf16),
            pltpu.VMEM((4, 8, 16, 256), bf16),
            pltpu.VMEM((3, 8, 16, 256), bf16),
            pltpu.VMEM((8, 16, 256), bf16),
            pltpu.VMEM((7, 16, 256), bf16),
            dma((STEPS,)),
            dma((STEPS,)),
            dma((STEPS,)),
            dma((STEPS,)),
            dma((STEPS,)),
            dma((11,)),
            dma((11,)),
            dma,
        ],
        compiler_params=pltpu.CompilerParams(
            collective_id=0, has_side_effects=True, vmem_limit_bytes=56 * 1024 * 1024
        ),
    )(
        volts, history, zoom_bins.reshape(FINE, FINE), counts.reshape(FINE, FINE),
        dft_rows(), pfb_taps, beam_stations, beam_weights,
    )
    split = power.reshape(2, 8, 2, 2, NT, 8)[:, :, :, 0, :, :NB]
    beam_power = split.transpose(4, 2, 1, 0, 3).reshape(NB, COARSE, 2, NT)
    return vis[None, None], beam_power


def solution(mesh):
    in_specs = (P("af", "gx", None, None), P("af", "gx", None, None), P(), P(), P(), P(), P())
    out_specs = (P("af", "gx", None, None), P(None, "gx", "af", None))
    return jax.shard_map(
        per_device, mesh=mesh, in_specs=in_specs, out_specs=out_specs, check_vma=False
    )
```

```python
import jax
import jax.numpy as jnp
import numpy as np
from jax import lax
from jax.experimental import pallas as pl
from jax.experimental.pallas import tpu as pltpu
from jax.sharding import PartitionSpec as P

FINE = 128
TAPS = 12
NT = 8
NB = 6
BINS = 64
GROUPS = 8
LOCAL = 16
COARSE = 16
CHG = 2048
NIN = 1024
LANES = 256
PAIRS = 4
PARTS = ((0, 1), (1, 1), (2, 2), (4, 2), (6, 2))
STEPS = len(PARTS)
MESH = pl.DeviceIdType.MESH
CONTRACT_LANES = (((1,), (1,)), ((), ()))


def dft_rows():
    index = np.arange(FINE)
    angle = (index[:, None] * index[None, :] % FINE) * (2.0 * np.pi / FINE)
    cosine = np.cos(angle) / np.sqrt(FINE)
    sine = np.sin(angle) / np.sqrt(FINE)
    return jnp.asarray(np.concatenate([cosine.T, sine.T], axis=1), jnp.bfloat16)


def to(device):
    return dict(device_id=device, device_id_type=MESH)


def iota(shape, dim):
    return lax.broadcasted_iota(jnp.int32, shape, dim)


def kernel(
    volts, history, zoom_bins, counts, table, taps, stations, beam_weights,
    acc_out, last, beam_out, scale_out,
    frames, filt, ysend, yrecv, place, pick, outgo, arrived, turned, acc,
    wraw, member, beams, beams2, bsend0, brecv0, bsend1, brecv1, bsend2, brecv2,
    frame_sem, ysend_sem, yrecv_sem, send_sem, recv_sem,
    bsend_sem, brecv_sem, own_sem, acc_sem,
):
    me = lax.axis_index("af")
    gx = lax.axis_index("gx")
    my_z = me // 8
    my_x = (me // 2) % 4
    my_core = me % 2
    my_low = me % 8
    f32, bf16 = jnp.float32, jnp.bfloat16

    barrier = pltpu.get_barrier_semaphore()

    def frame_range(step):
        first, count = PARTS[step]
        return (first + TAPS - 1 if step else 0), first + count + TAPS - 1

    def fetch_step(step):
        def one(i, carry):
            for f in range(*frame_range(step)):
                if f < TAPS - 1:
                    source = history.at[i, :, :, f * FINE : (f + 1) * FINE]
                else:
                    source = volts.at[i, :, :, (f - TAPS + 1) * FINE : (f - TAPS + 2) * FINE]
                pltpu.make_async_copy(source, frames.at[f, :, pl.ds(2 * i, 2)], frame_sem.at[step]).start()
            return carry

        lax.fori_loop(0, LOCAL, one, 0)

    fetch_step(0)

    def greet(d, carry):
        pl.semaphore_signal(barrier, inc=1, **to({"af": (me + d) % BINS}))
        return carry

    lax.fori_loop(1, BINS, greet, 0)

    def greet_gx(d, carry):
        pl.semaphore_signal(barrier, inc=1, **to({"gx": (gx + d) % GROUPS}))
        return carry

    lax.fori_loop(1, GROUPS, greet_gx, 0)
    for step in range(1, STEPS):
        fetch_step(step)

    def channelize(step):
        first, count = PARTS[step]
        start, stop = frame_range(step)
        arrived_now = frames.at[start:stop]
        pltpu.make_async_copy(arrived_now, arrived_now, frame_sem.at[step]).wait()

        def bank(c, carry):
            for part in range(2):
                rows = slice(part * LOCAL, (part + 1) * LOCAL)
                x = [frames[first + j, c, rows, :].astype(f32) for j in range(TAPS + count - 1)]
                for t in range(count):
                    total = x[t] * taps[0:1, :]
                    for j in range(1, TAPS):
                        total = total + x[t + j] * taps[j : j + 1, :]
                    filt[c, t * 32 + part * LOCAL : t * 32 + (part + 1) * LOCAL, :] = total
            return carry

        lax.fori_loop(0, COARSE, bank, 0, unroll=2)
        span = 4 * count

        def transform(u, carry):
            blocks = []
            for cp in range(2):
                for q in range(COARSE // span):
                    c = 2 * u + cp + span * q
                    re = filt[c, pl.ds(0, count * LOCAL, stride=2), :].astype(bf16)
                    im = filt[c, pl.ds(1, count * LOCAL, stride=2), :].astype(bf16)
                    blocks.append(jnp.concatenate([re, im], axis=1))
                    blocks.append(jnp.concatenate([im, -re], axis=1))
            rows = jnp.concatenate(blocks, axis=0)
            spectra = lax.dot_general(table[...], rows, CONTRACT_LANES, preferred_element_type=f32).astype(bf16)
            for cp in range(2):
                ysend[first // 2, :, 4 * (first % 2) + 2 * u + cp] = spectra[
                    :, cp * FINE : (cp + 1) * FINE
                ].reshape(GROUPS, 16, FINE)
            return carry

        lax.fori_loop(0, span // 2, transform, 0, unroll=2)

    def y_part(ref, step, who):
        first, count = PARTS[step]
        return ref.at[first // 2, who, pl.ds(4 * (first % 2), 4 * count)]

    def send_spectra(step):
        first, count = PARTS[step]

        def one(d, carry):
            dest = (gx + d) % GROUPS
            pltpu.make_async_remote_copy(
                src_ref=y_part(ysend, step, dest),
                dst_ref=y_part(yrecv, step, gx),
                send_sem=ysend_sem.at[step],
                recv_sem=yrecv_sem.at[step],
                **to({"gx": dest}),
            ).start()
            return carry

        lax.fori_loop(1, GROUPS, one, 0)
        rows = slice(4 * (first % 2), 4 * (first % 2) + 4 * count)
        yrecv[first // 2, gx, rows] = ysend[first // 2, gx, rows]

    channelize(0)
    pl.semaphore_wait(barrier, BINS - 1 + GROUPS - 1)
    send_spectra(0)
    channelize(1)
    send_spectra(1)
    channelize(2)
    send_spectra(2)

    my_rows = pl.ds(pl.multiple_of(gx * 16, 16), 16)
    bins_here = zoom_bins[my_rows, :]
    counts_here = counts[my_rows, :]
    in_bin = jnp.where(bins_here == me, counts_here.astype(f32), 0.0)
    in_bin = jnp.sum(jnp.sum(in_bin, axis=1, keepdims=True), axis=0, keepdims=True)
    scale_out[...] = jnp.broadcast_to(1.0 / jnp.maximum(in_bin, 1.0), (8, FINE))
    bins_down = bins_here.astype(f32).T
    lane = iota((FINE, FINE), 1)
    lane_f = lane.astype(f32)
    lower = (lane < iota((FINE, FINE), 0)).astype(f32).astype(bf16)
    ones = jnp.ones((FINE, FINE), bf16)
    seen = jnp.zeros((1, FINE), f32)
    for block in range(16):
        upper, y = block // 8, block % 8
        row = 2 * y + upper
        column = jnp.broadcast_to(bins_down[:, row : row + 1], (FINE, FINE))
        hits = (column == lane_f).astype(f32)
        before = jnp.dot(lower, hits.astype(bf16), preferred_element_type=f32) + seen
        seen = seen + jnp.sum(hits, axis=0, keepdims=True)
        rank = jnp.dot((hits * before).astype(bf16), ones, preferred_element_type=f32)
        pair = jnp.floor(column * 0.5)
        slot = (column - 2.0 * pair) * 64.0 + rank
        place[block * FINE : (block + 1) * FINE, :] = jnp.where(slot == lane_f, pair, -1.0).astype(bf16)

    def spread(z, carry):
        for p in range(4):
            here = (z * 4 + p).astype(f32).astype(bf16)
            pick[z, :, p * FINE : (p + 1) * FINE] = jnp.where(
                place[...] == here, jnp.ones((), bf16), jnp.zeros((), bf16)
            )
        return carry

    lax.fori_loop(0, 8, spread, 0)
    own_rows = pl.ds(pl.multiple_of(me * LOCAL, LOCAL), LOCAL)

    def landing(step, rows):
        first, count = PARTS[step]
        cols = slice((first % 2) * FINE, (first % 2 + count) * FINE)
        if first // 2 == PAIRS - 1:
            return last.at[rows]
        return arrived.at[first // 2, rows, cols]

    def leaving(step, who):
        first, count = PARTS[step]
        cols = slice((first % 2) * FINE, (first % 2 + count) * FINE)
        return outgo.at[first // 2, who, :, cols]

    def distribute(step):
        first, count = PARTS[step]
        pair = first // 2
        others = y_part(yrecv, step, pl.ds(0, GROUPS - 1))
        pltpu.make_async_copy(others, others, yrecv_sem.at[step]).wait()
        spectrum = first + (iota((count * 32, FINE), 0) // LOCAL) % count
        cells = [[], []]
        for y in range(GROUPS):
            rows = slice(4 * (first % 2), 4 * (first % 2) + 4 * count)
            samples = yrecv[pair, y, rows].reshape(64 * count, FINE).astype(f32).T
            for upper in range(2):
                if count == 2:
                    cell = samples[upper * 64 : (upper + 1) * 64]
                else:
                    cell = jnp.concatenate(
                        [samples[q * 32 : (q + 1) * 32] for q in (2 * upper, 2 * upper + 1)], axis=1
                    )
                keep = spectrum < counts_here[2 * y + upper : 2 * y + upper + 1, :]
                cells[upper].append(jnp.where(keep, cell, 0.0).astype(bf16))
        flipped = jnp.concatenate(cells[0] + cells[1], axis=1)
        low = iota((LOCAL, FINE), 1) < 64

        def one(turn, carry):
            turn = 7 - turn
            hop = ((turn + 1) // 2) * (2 * (turn % 2) - 1)
            z = (my_z + hop + 8) % 8
            picked = jnp.dot(flipped, pick[z], preferred_element_type=f32)
            for b in range(4):
                for t in range(count):
                    lanes = slice(b * FINE, (b + 1) * FINE)
                    re = picked[t * 16 : t * 16 + 16, lanes]
                    im = picked[(count + t) * 16 : (count + t) * 16 + 16, lanes]
                    im = pltpu.roll(im, 64, 1)
                    cols = slice((first % 2 + t) * FINE, (first % 2 + t + 1) * FINE)
                    outgo[pair, z * 8 + 2 * b, :, cols] = jnp.where(low, re, im).astype(bf16)
                    outgo[pair, z * 8 + 2 * b + 1, :, cols] = jnp.where(low, im, re).astype(bf16)

            def send(k, c):
                dest = z * 8 + (my_low + k) % 8

                @pl.when(dest != me)
                def _():
                    pltpu.make_async_remote_copy(
                        src_ref=leaving(step, dest),
                        dst_ref=landing(step, own_rows),
                        send_sem=send_sem.at[step],
                        recv_sem=recv_sem.at[step],
                        **to({"af": dest}),
                    ).start()

                return c

            lax.fori_loop(0, 8, send, 0)
            return carry

        lax.fori_loop(0, 8, one, 0, unroll=8)
        if pair < PAIRS - 1:
            cols = slice((first % 2) * FINE, (first % 2 + count) * FINE)
            arrived[pair, own_rows, cols] = outgo[pair, me, :, cols]
        else:
            pltpu.make_async_copy(outgo.at[pair, me], last.at[own_rows], own_sem).start()

    def await_part(step):
        others = landing(step, pl.ds(0, (BINS - 1) * LOCAL))
        pltpu.make_async_copy(others, others, recv_sem.at[step]).wait()

    distribute(0)
    distribute(1)
    channelize(3)
    send_spectra(3)
    channelize(4)
    send_spectra(4)
    distribute(2)

    lanes6 = iota((NB, FINE), 1)
    found = jnp.zeros((NB, FINE), f32)
    for st in range(LOCAL // 2):
        here = jnp.sum((stations[...] == me * (LOCAL // 2) + st).astype(f32), axis=1, keepdims=True)
        found = jnp.where(lanes6 // 2 == st, here, found)
    wraw[...] = jnp.zeros_like(wraw)
    member[...] = jnp.zeros_like(member)
    near = pl.ds(pl.multiple_of((me // 8) * FINE, FINE), FINE)
    for p in range(2):
        member[p * 8 : p * 8 + NB, :] = found
        for b in range(NB):
            wraw[p * 8 + b : p * 8 + b + 1, :] = beam_weights[b, p : p + 1, near]
    by_beam = (member[...] * pltpu.roll(wraw[...], (FINE - my_low * LOCAL) % FINE, 1)).astype(bf16)

    def spread_weights(height, width, s_of, t_of, q_of):
        row, col = iota((height, width), 0), iota((height, width), 1)
        by_input = (iota((height, FINE), 1) == iota((height, FINE), 0) % LOCAL).astype(f32).astype(bf16)
        chosen = lax.dot_general(by_input, by_beam, CONTRACT_LANES, preferred_element_type=f32).astype(bf16)
        wide_row, wide_lane = iota((16, width), 0), iota((16, width), 1)
        beam = (wide_lane // 8) % 8
        wre = jnp.dot(chosen, (wide_row == beam).astype(f32).astype(bf16), preferred_element_type=f32)
        wim = jnp.dot(chosen, (wide_row == 8 + beam).astype(f32).astype(bf16), preferred_element_type=f32)
        same = jnp.logical_and(q_of(row) == col // FINE, t_of(row) == col % 8)
        mixed = jnp.where(s_of(row) == (col // 64) % 2, wre, jnp.where(s_of(row) == 0, wim, -wim))
        return jnp.where(same, mixed, 0.0).astype(bf16)

    early_weights = spread_weights(
        256, 512, lambda r: (r // 16) % 2, lambda r: r // 128, lambda r: (r // 32) % 4
    )
    late_weights = spread_weights(
        384, 256, lambda r: (r // 32) % 2, lambda r: 2 + 2 * (r // 128) + (r // 16) % 2, lambda r: (r // 64) % 2
    )
    for z in range(8):
        spectra = jnp.concatenate([ysend[p, z].reshape(FINE, FINE) for p in range(1, PAIRS)], axis=1)
        late = jnp.dot(spectra, late_weights, preferred_element_type=f32)
        spectra = jnp.concatenate([ysend[0, z, 4 * t : 4 * t + 4].reshape(64, FINE) for t in range(2)], axis=1)
        early = jnp.dot(spectra, early_weights, preferred_element_type=f32)
        for h in range(2):
            for low in range(2):
                rows = slice(low * 64, (low + 1) * 64)
                q = 2 * h + low
                beams[h, rows, :] = late[rows, h * FINE : (h + 1) * FINE] + early[:, q * FINE : (q + 1) * FINE]
        for x in range(4):
            for core in range(2):
                for e in range(2):
                    for h in range(2):
                        beams2[z, x, core, e * 8 : e * 8 + 8, h * FINE : (h + 1) * FINE] = beams[
                            h, pl.ds(x * 4 + core * 2 + e, 8, stride=16), :
                        ]

    def pack0(s, carry):
        bsend0[s] = beams2[s // 4, s % 4, 1 - my_core].astype(bf16)
        return carry

    lax.fori_loop(0, 32, pack0, 0)
    sibling = my_z * 8 + my_x * 2 + 1 - my_core
    core_copy = pltpu.make_async_remote_copy(
        src_ref=bsend0, dst_ref=brecv0, send_sem=bsend_sem.at[0], recv_sem=brecv_sem.at[0],
        **to({"af": sibling}),
    )
    core_copy.start()

    distribute(3)

    core_copy.wait()

    def pack1(s, carry):
        total = beams2[s // 4, s % 4, my_core] + brecv0[s].astype(f32)
        beams2[s // 4, s % 4, my_core] = total
        bsend1[s % 4, s // 4] = total.astype(bf16)
        return carry

    lax.fori_loop(0, 32, pack1, 0)
    x_copies = []
    for d in range(1, 4):
        x = (my_x + d) % 4
        x_copies.append(
            pltpu.make_async_remote_copy(
                src_ref=bsend1.at[x], dst_ref=brecv1.at[d - 1],
                send_sem=bsend_sem.at[d], recv_sem=brecv_sem.at[d],
                **to({"af": my_z * 8 + x * 2 + my_core}),
            )
        )
        x_copies[-1].start()

    distribute(4)

    for copy in x_copies:
        copy.wait()

    def pack2(zz, carry):
        total = beams2[zz, my_x, my_core]
        for d in range(3):
            total = total + brecv1[d, zz].astype(f32)
        beams2[zz, my_x, my_core] = total
        bsend2[zz] = total.astype(bf16)
        return carry

    lax.fori_loop(0, 8, pack2, 0)
    z_copies = []
    for d in range(1, 8):
        zz = (my_z + d) % 8
        z_copies.append(
            pltpu.make_async_remote_copy(
                src_ref=bsend2.at[zz], dst_ref=brecv2.at[d - 1],
                send_sem=bsend_sem.at[3 + d], recv_sem=brecv_sem.at[3 + d],
                **to({"af": zz * 8 + my_low}),
            )
        )
        z_copies[-1].start()

    def correlate(pair, fresh):
        turn_over(arrived.at[pair], turned, my_core)

        def keep(bi, bj, value):
            acc[bi, bj] = value if fresh else acc[bi, bj] + value

        products(arrived.at[pair], turned, keep)

    await_part(0)
    await_part(1)
    correlate(0, True)
    await_part(2)
    correlate(1, False)
    await_part(3)
    correlate(2, False)
    acc_copy = pltpu.make_async_copy(acc, acc_out, acc_sem)
    acc_copy.start()

    for copy in z_copies:
        copy.wait()
    total = beams2[my_z, my_x, my_core]
    for d in range(7):
        total = total + brecv2[d].astype(f32)
    beam_out[...] = total

    for step in range(STEPS):
        others = y_part(ysend, step, pl.ds(0, GROUPS - 1))
        pltpu.make_async_copy(others, others, ysend_sem.at[step]).wait()
        others = leaving(step, pl.ds(0, BINS - 1))
        pltpu.make_async_copy(others, others, send_sem.at[step]).wait()
    acc_copy.wait()
    pltpu.make_async_copy(outgo.at[PAIRS - 1, me], last.at[own_rows], own_sem).wait()
    await_part(STEPS - 1)


def turn_over(source, target, core):
    sign = jnp.where(iota((256, FINE), 1) < 64, 1.0, -1.0) * (1 - 2 * core).astype(jnp.float32)
    for bi in range(4):
        for t in range(2):
            rows, cols = slice(bi * 256, (bi + 1) * 256), slice(t * FINE, (t + 1) * FINE)
            swapped = pltpu.roll(source[rows, cols].astype(jnp.float32), 64, 1)
            target[rows, cols] = (swapped * sign).astype(jnp.bfloat16)


def products(plain, turned, keep):
    diagonal = iota((256, 256), 1) >= iota((256, 256), 0)
    for bi in range(4):
        rows = slice(bi * 256, (bi + 1) * 256)
        for bj in range(4):
            right = plain[bj * 256 : (bj + 1) * 256, :]
            if bj >= bi:
                real = lax.dot_general(plain[rows, :], right, CONTRACT_LANES, preferred_element_type=jnp.float32)
            if bj <= bi:
                imag = lax.dot_general(turned[rows, :], right, CONTRACT_LANES, preferred_element_type=jnp.float32)
            if bj > bi:
                value = real
            elif bj < bi:
                value = imag
            else:
                value = jnp.where(diagonal, real, imag)
            keep(bi, bj, value)


def finish(acc_in, last_in, beam_in, scale, vis, power, acc, last, turned, visbuf, acc_sem, last_sem, vis_sem):
    last_copy = pltpu.make_async_copy(last_in, last, last_sem)
    last_copy.start()
    acc_copies = [pltpu.make_async_copy(acc_in.at[b], acc.at[b], acc_sem.at[b]) for b in range(4)]
    for copy in acc_copies:
        copy.start()
    total = beam_in[...]
    square = total * total
    halves = [square[:, h * FINE : (h + 1) * FINE] for h in range(2)]
    halves = [half + pltpu.roll(half, 64, 1) for half in halves]
    for e in range(2):
        rows = slice(e * 8, (e + 1) * 8)
        by_time = jnp.concatenate([half[rows] for half in halves], axis=0).T
        for b in range(NB):
            power[b, e] = by_time[b * 8 : (b + 1) * 8, :]
    last_copy.wait()
    turn_over(last, turned, lax.axis_index("af") % 2)
    vis_copies = []

    def keep(bi, bj, value):
        if bj == 0:
            acc_copies[bi].wait()
        rows, cols = slice(bi * 256, (bi + 1) * 256), slice(bj * 256, (bj + 1) * 256)
        visbuf[rows, cols] = ((acc[bi, bj] + value) * scale[0:1, 0:1]).astype(jnp.bfloat16)
        if bj == 3:
            vis_copies.append(pltpu.make_async_copy(visbuf.at[rows], vis.at[rows], vis_sem.at[bi]))
            vis_copies[-1].start()

    products(last, turned, keep)
    for copy in vis_copies:
        copy.wait()


def per_device(volts, history, pfb_taps, zoom_bins, counts, beam_stations, beam_weights):
    vmem = pl.BlockSpec(memory_space=pltpu.VMEM)
    hbm = pl.BlockSpec(memory_space=pl.ANY)
    bf16, f32 = jnp.bfloat16, jnp.float32
    dma = pltpu.SemaphoreType.DMA
    acc, last, beam, scale = pl.pallas_call(
        kernel,
        out_shape=[
            jax.ShapeDtypeStruct((4, 4, 256, 256), f32),
            jax.ShapeDtypeStruct((NIN, LANES), bf16),
            jax.ShapeDtypeStruct((16, 2 * FINE), f32),
            jax.ShapeDtypeStruct((8, FINE), f32),
        ],
        in_specs=[hbm, hbm, vmem, vmem, vmem, vmem, vmem, vmem],
        out_specs=[hbm, hbm, vmem, vmem],
        scratch_shapes=[
            pltpu.VMEM((NT + TAPS - 1, COARSE, 2 * LOCAL, FINE), bf16),
            pltpu.VMEM((COARSE, 64, FINE), f32),
            pltpu.VMEM((PAIRS, GROUPS, 8, 16, FINE), bf16),
            pltpu.VMEM((PAIRS, GROUPS, 8, 16, FINE), bf16),
            pltpu.VMEM((CHG, FINE), bf16),
            pltpu.VMEM((8, CHG, 512), bf16),
            pltpu.VMEM((PAIRS, BINS, LOCAL, LANES), bf16),
            pltpu.VMEM((PAIRS - 1, NIN, LANES), bf16),
            pltpu.VMEM((NIN, LANES), bf16),
            pltpu.VMEM((4, 4, 256, 256), f32),
            pltpu.VMEM((16, FINE), f32),
            pltpu.VMEM((16, FINE), f32),
            pltpu.VMEM((2, FINE, FINE), f32),
            pltpu.VMEM((8, 4, 2, 16, 256), f32),
            pltpu.VMEM((32, 16, 256), bf16),
            pltpu.VMEM((32, 16, 256), bf16),
            pltpu.VMEM((4, 8, 16, 256), bf16),
            pltpu.VMEM((3, 8, 16, 256), bf16),
            pltpu.VMEM((8, 16, 256), bf16),
            pltpu.VMEM((7, 16, 256), bf16),
            dma((STEPS,)),
            dma((STEPS,)),
            dma((STEPS,)),
            dma((STEPS,)),
            dma((STEPS,)),
            dma((11,)),
            dma((11,)),
            dma,
            dma,
        ],
        compiler_params=pltpu.CompilerParams(
            collective_id=0, has_side_effects=True, vmem_limit_bytes=56 * 1024 * 1024
        ),
    )(
        volts, history, zoom_bins.reshape(FINE, FINE), counts.reshape(FINE, FINE),
        dft_rows(), pfb_taps, beam_stations, beam_weights.transpose(1, 0, 2),
    )
    vis, power = pl.pallas_call(
        finish,
        out_shape=[
            jax.ShapeDtypeStruct((NIN, NIN), bf16),
            jax.ShapeDtypeStruct((NB, 2, NT, COARSE), f32),
        ],
        in_specs=[hbm, hbm, vmem, vmem],
        out_specs=[hbm, vmem],
        scratch_shapes=[
            pltpu.VMEM((4, 4, 256, 256), f32),
            pltpu.VMEM((NIN, LANES), bf16),
            pltpu.VMEM((NIN, LANES), bf16),
            pltpu.VMEM((NIN, NIN), bf16),
            dma((4,)),
            dma,
            dma((4,)),
        ],
        compiler_params=pltpu.CompilerParams(vmem_limit_bytes=58 * 1024 * 1024),
    )(acc, last, beam, scale)
    return vis[None, None], power.transpose(0, 3, 1, 2)


def solution(mesh):
    in_specs = (P("af", "gx", None, None), P("af", "gx", None, None), P(), P(), P(), P(), P())
    out_specs = (P("af", "gx", None, None), P(None, "gx", "af", None))
    return jax.shard_map(
        per_device, mesh=mesh, in_specs=in_specs, out_specs=out_specs, check_vma=False
    )
```
